32 devices in a mesh: groups: 2 (over x), gx: 16 (over z, y, core).
Axes of the slice: x: 2, y: 2, z: 4, core: 2. Of those that a mesh axis runs over, the one named last changes fastest.
Arguments:
- features: bfloat16 [64, 98304], P(None, ('groups', 'gx')), parts along dimension 1, may hold values from -6 to 6
- cotangent: bfloat16 [64, 98304], P(None, ('groups', 'gx')), parts along dimension 1, may hold values from -6 to 6
- weights: bfloat16 [27, 64, 64], replicated, may hold values from -0.15625 to 0.15625
- kernel_map: int32 [27, 98304], P(None, ('groups', 'gx')), parts along dimension 1, may hold values from 0 to 5120, as said below
- interior_bricks: int32 [32], P(('groups', 'gx')), parts along dimension 0, may hold values from 0 to 8, as said below
Outputs:
- output: bfloat16 [64, 98304], P(None, ('groups', 'gx')), parts along dimension 1
- grad_features: bfloat16 [64, 98304], P(None, ('groups', 'gx')), parts along dimension 1
- grad_weights: float32 [54, 64, 64], P('groups'), parts along dimension 0
The draws below stay inside these ranges and needn't reach their ends.
There are 2 independent parts, one for each index of `groups`. The reference program is written for one: setup_inputs(seed, part) draws one part's arguments, and reference() takes and returns one part's arrays. A program takes and returns all parts, laid end to end along the dimension named above; an argument that names none is the same for every part. Nothing has to cross between parts.
Inputs may be any that keep to these rules, and one draw needn't show every extreme that they name: Offsets are ordered k = 9 (dx + 1) + 3 (dy + 1) + (dz + 1). A voxel's sources lie on its own device or in the outermost 8 bricks of an adjacent device; a value of 5120 means no source. The maps are symmetric: where kernel_map[k, v] names voxel w, kernel_map[26 - k, w] names v. Voxels that are not live have no sources and are no one's source. `interior_bricks`: the occupied inner bricks of a device fill the slots right after its first 8; the other inner slots are empty.
All inputs are finite; a program needn't handle non-finite values.
Results may differ from the reference program's by a relative error of at most 0.0025.
Values may be sent and summed in bfloat16 or wider, within the bound.
A program may use at most 128 MiB of HBM per device.

```python
import jax
import jax.numpy as jnp
from jax import lax

C = 64
BY = 2
BZ = 4
LAYERS = 3
RB = 8
NB = 24
VOX_DEV = 3072
VOXELS = 49152
N_GX = 16


def brick_layout(key):
    key = jax.random.fold_in(key, 11)
    key_count, key_device, key_perm, key_voxel = jax.random.split(key, 4)
    inner_total = (LAYERS - 2) * RB
    devices = jnp.arange(N_GX, dtype=jnp.int32)
    counts = jax.random.randint(key_count, (N_GX,), 0, inner_total + 1).astype(jnp.int32)
    fullest = jax.random.randint(key_device, (), 0, N_GX).astype(jnp.int32)
    counts = jnp.where(devices == fullest, inner_total, counts).astype(jnp.int32)
    ranking = jax.vmap(lambda sub_key: jax.random.permutation(sub_key, inner_total))(jax.random.split(key_perm, N_GX))
    present = ranking < counts[:, None]
    rank_in = jnp.cumsum(present.astype(jnp.int32), axis=1) - 1
    inner_slots = jnp.where(present, RB + rank_in, -1).reshape(N_GX, LAYERS - 2, RB).astype(jnp.int32)
    face_ids = jnp.arange(RB, dtype=jnp.int32)
    first_face = jnp.broadcast_to(face_ids, (N_GX, 1, RB))
    last_face = jnp.broadcast_to(NB - RB + face_ids, (N_GX, 1, RB))
    slots = jnp.concatenate([first_face, inner_slots, last_face], axis=1)
    occupied_bits = jax.random.randint(key_voxel, (N_GX, LAYERS, RB, 128), 0, 2).astype(jnp.int32)
    placed = (devices[:, None, None, None] * NB + slots[..., None]) * 128 + jnp.arange(128, dtype=jnp.int32)[None, None, None, :]
    stored = jnp.where((occupied_bits == 1) & (slots[..., None] >= 0), placed, -1).astype(jnp.int32)
    voxel_grid = stored.reshape(N_GX, LAYERS, BY, BZ, 4, 4, 8).transpose(0, 1, 4, 2, 5, 3, 6).reshape(N_GX * LAYERS * 4, BY * 4, BZ * 8)
    size_x, size_y, size_z = voxel_grid.shape
    padded = jnp.pad(voxel_grid, 1, constant_values=-1)
    nearby = []
    for step_x in (-1, 0, 1):
        for step_y in (-1, 0, 1):
            for step_z in (-1, 0, 1):
                window = padded[1 + step_x:1 + step_x + size_x, 1 + step_y:1 + step_y + size_y, 1 + step_z:1 + step_z + size_z]
                nearby.append(window.reshape(-1))
    nearby = jnp.stack(nearby)
    flattened = voxel_grid.reshape(-1)
    targets = jnp.where(flattened >= 0, flattened, VOXELS).astype(jnp.int32)
    lookup = jnp.full((27, VOXELS), -1, jnp.int32).at[:, targets].set(nearby, mode='drop')
    owners = jnp.arange(VOXELS, dtype=jnp.int32) // (NB * 128)
    kernel_ext = jnp.where(lookup >= 0, lookup - owners[None, :] * (NB * 128) + RB * 128, (NB + 2 * RB) * 128)
    return (kernel_ext.astype(jnp.int32), counts)


def draw_kernel_map(key, part):
    kernel_ext, counts = brick_layout(key)
    return kernel_ext


def draw_interior_bricks(key, part):
    kernel_ext, counts = brick_layout(key)
    return counts


def block_scale(rng, dims, cuts, smallest, top_value):
    loudness, own = 1.0, jax.random.fold_in(rng, 6)
    for position, shards_of in cuts:
        draws = jnp.exp(jax.random.uniform(jax.random.fold_in(own, position), (shards_of,), jnp.float32, smallest / len(cuts), top_value / len(cuts)))
        loudness = loudness * jnp.repeat(draws, dims[position] // shards_of).reshape([-1 if axis == position else 1 for axis in range(len(dims))])
    return loudness


def bell_draw(rng, dims, deviation, most, shards=(), kind=jnp.bfloat16):
    array = deviation * jax.random.normal(rng, dims, jnp.float32)
    if shards:
        array = array * block_scale(rng, dims, shards, -0.22, 0.18)
    return jnp.clip(array, -most, most).astype(kind)


def setup_inputs(seed: int = 0, part: int = 0) -> dict:
    seeds = jax.random.split(jax.random.key(seed), 6)
    part_keys = jax.random.split(jax.random.fold_in(seeds[5], part), 6)
    return {
        "features": bell_draw(part_keys[0], (C, VOXELS), 1.0, 6.0, ((1, 16),)),
        "cotangent": bell_draw(part_keys[1], (C, VOXELS), 1.0, 6.0, ((1, 16),)),
        "weights": bell_draw(seeds[2], (27, C, C), (27 * C) ** -0.5, 0.15625),
        "kernel_map": draw_kernel_map(jax.random.fold_in(jax.random.fold_in(seeds[5], part), 71), part),
        "interior_bricks": draw_interior_bricks(jax.random.fold_in(jax.random.fold_in(seeds[5], part), 71), part),
    }


def reference(features, cotangent, weights, kernel_map, interior_bricks):
    rim_len = RB * 128
    voxel_ids = jnp.arange(VOXELS, dtype=jnp.int32)
    slot_ids = (voxel_ids // 128) % NB
    owners = voxel_ids // VOX_DEV
    live = (slot_ids < RB) | (slot_ids >= NB - RB) | (slot_ids - RB < interior_bricks[owners])
    masked_up = jnp.where(live[None, :], cotangent, jnp.zeros_like(cotangent))
    padded_features = jnp.pad(features, ((0, 0), (rim_len, rim_len)))
    padded_upstream = jnp.pad(masked_up, ((0, 0), (rim_len, rim_len)))
    weights_wide = weights.astype(jnp.float32)

    def per_device(weight_sum, device_id):
        begin = (device_id * VOX_DEV).astype(jnp.int32)
        feature_ext = lax.dynamic_slice_in_dim(padded_features, begin, VOX_DEV + 2 * rim_len, 1).astype(jnp.float32)
        upstream_ext = lax.dynamic_slice_in_dim(padded_upstream, begin, VOX_DEV + 2 * rim_len, 1).astype(jnp.float32)
        indices = lax.dynamic_slice_in_dim(kernel_map, begin, VOX_DEV, 1)
        live_part = lax.dynamic_slice_in_dim(live, begin, VOX_DEV, 0)[None, :]
        picked = jnp.take(feature_ext, indices, axis=1, mode="fill", fill_value=0.0)
        result = jnp.einsum("kab,bkv->av", weights_wide, picked)
        result = jnp.where(live_part, result, 0.0).astype(jnp.bfloat16)
        gathered_up = jnp.take(upstream_ext, indices[::-1], axis=1, mode="fill", fill_value=0.0)
        input_part = jnp.einsum("kab,akv->bv", weights_wide, gathered_up)
        input_part = jnp.where(live_part, input_part, 0.0).astype(jnp.bfloat16)
        upstream_own = lax.dynamic_slice_in_dim(masked_up, begin, VOX_DEV, 1).astype(jnp.float32)
        weight_sum = weight_sum + jnp.einsum("av,bkv->kab", upstream_own, picked)
        return weight_sum, (result, input_part)

    weight_sum, (results, input_parts) = lax.scan(per_device, jnp.zeros((27, C, C), jnp.float32), jnp.arange(N_GX, dtype=jnp.int32))
    output = jnp.transpose(results, (1, 0, 2)).reshape(C, VOXELS)
    grad_features = jnp.transpose(input_parts, (1, 0, 2)).reshape(C, VOXELS)
    grad_weights = weight_sum * (float(VOXELS) ** -0.5)
    return output, grad_features, grad_weights
```

```python
import functools

import jax
import jax.numpy as jnp
from jax import lax
from jax.experimental import pallas as pl
from jax.experimental.pallas import tpu as pltpu
from jax.sharding import PartitionSpec as P

RB = 8
BRICK = 128
ROWS = 256


def gather_kernel(
    taps, channels, own_len, factor,
    flags, index, filled,
    feat, cot, left, right, stack,
    out_ref, gf_ref, gw_ref,
    picked, table, block, ups, compact, result,
):
    rim_len = RB * BRICK
    wide = 2 * channels
    none = own_len + 2 * rim_len
    bricks = own_len // BRICK

    def fill_table(start, tile):
        table[pl.ds(start, BRICK), :] = tile.astype(jnp.float32).T

    for b in range(RB):
        cols = slice(b * BRICK, (b + 1) * BRICK)
        fill_table(b * BRICK, left[:, cols])
        fill_table(rim_len + own_len + b * BRICK, right[:, cols])
    for b in range(bricks):
        cols = slice(b * BRICK, (b + 1) * BRICK)
        up = cot[:, cols].astype(jnp.float32)
        if RB <= b < bricks - RB:
            up = jnp.where(b - RB < filled[0], up, 0.0)
        own = jnp.concatenate([feat[:, cols].astype(jnp.float32), up], axis=0)
        fill_table(rim_len + b * BRICK, own)
    table[pl.ds(none, 8), :] = jnp.zeros((8, wide), jnp.float32)
    result[...] = jnp.zeros_like(result)
    gw_ref[...] = jnp.zeros_like(gw_ref)

    def note(step, count):
        for j in range(16):
            voxel = step * 16 + j
            picked[count] = voxel
            count = count + flags[voxel]
        return count

    count = lax.fori_loop(0, own_len // 16, note, 0)

    def pad(i, _):
        picked[count + i] = 0
        return _

    lax.fori_loop(0, ROWS, pad, 0)

    def visit(blk, _):
        base = blk * ROWS

        def fetch(step, _):
            for j in range(8):
                voxel = picked[base + step * 8 + j]
                ups[step, j : j + 1, :] = table[pl.ds(voxel + rim_len, 1), :]
                for k in range(taps):
                    source = index[k * own_len + voxel]
                    block[step, j : j + 1, k * wide : (k + 1) * wide] = table[pl.ds(source, 1), :]
            return _

        lax.fori_loop(0, ROWS // 8, fetch, 0)
        up = ups[...].reshape(ROWS, wide)
        row = lax.broadcasted_iota(jnp.int32, (ROWS, wide), 0)
        up = jnp.where(row + base < count, up, 0.0)
        up = up.T[channels:].astype(jnp.bfloat16)
        total = jnp.zeros((ROWS, wide), jnp.float32)
        for k in range(0, taps, 2):
            many = min(2, taps - k)
            cols = slice(k * wide, (k + many) * wide)
            part = block[:, :, cols].reshape(ROWS, many * wide).astype(jnp.bfloat16)
            total += jnp.dot(part, stack[cols, :], preferred_element_type=jnp.float32)
            grad = jnp.dot(up, part, preferred_element_type=jnp.float32)
            for m in range(many):
                gw_ref[k + m] += grad[:, m * wide : m * wide + channels]
        compact[pl.ds(pl.multiple_of(base, ROWS), ROWS), :] = total
        return _

    lax.fori_loop(0, (count + ROWS - 1) // ROWS, visit, 0)
    gw_ref[...] = gw_ref[...] * factor

    def place(step, _):
        for j in range(8):
            at = step * 8 + j
            result[pl.ds(picked[at], 1), :] = compact[pl.ds(at, 1), :]
        return _

    lax.fori_loop(0, count // 8, place, 0)

    def place_one(at, _):
        result[pl.ds(picked[at], 1), :] = compact[pl.ds(at, 1), :]
        return _

    lax.fori_loop(count // 8 * 8, count, place_one, 0)

    for b in range(bricks):
        cols = slice(b * BRICK, (b + 1) * BRICK)
        both = result[cols, :].T
        if RB <= b < bricks - RB:
            both = jnp.where(b - RB < filled[0], both, 0.0)
        out_ref[:, cols] = both[:channels].astype(jnp.bfloat16)
        gf_ref[:, cols] = both[channels:].astype(jnp.bfloat16)


def per_device(features, cotangent, weights, kernel_map, interior_bricks):
    channels, own_len = features.shape
    taps = weights.shape[0]
    rim_len = RB * BRICK
    wide = 2 * channels
    count = lax.axis_size("gx")
    none = own_len + 2 * rim_len
    factor = float(count * own_len) ** (-0.5)

    tail = jnp.concatenate([features[:, own_len - rim_len :], cotangent[:, own_len - rim_len :]], 0)
    head = jnp.concatenate([features[:, :rim_len], cotangent[:, :rim_len]], 0)
    left = lax.ppermute(tail, "gx", [(i, i + 1) for i in range(count - 1)])
    right = lax.ppermute(head, "gx", [(i + 1, i) for i in range(count - 1)])
    flags = jnp.any(kernel_map != none, axis=0).astype(jnp.int32)
    zero = jnp.zeros_like(weights)
    stack = jnp.concatenate(
        [
            jnp.concatenate([jnp.transpose(weights, (0, 2, 1)), zero], 2),
            jnp.concatenate([zero, weights[::-1]], 2),
        ],
        1,
    ).reshape(taps * wide, wide)
    smem = pl.BlockSpec(memory_space=pltpu.SMEM)
    vmem = pl.BlockSpec(memory_space=pltpu.VMEM)
    output, grad_features, partial = pl.pallas_call(
        functools.partial(gather_kernel, taps, channels, own_len, factor),
        out_shape=(
            jax.ShapeDtypeStruct((channels, own_len), jnp.bfloat16),
            jax.ShapeDtypeStruct((channels, own_len), jnp.bfloat16),
            jax.ShapeDtypeStruct((taps, channels, channels), jnp.float32),
        ),
        in_specs=[smem] * 3 + [vmem] * 5,
        out_specs=(vmem,) * 3,
        scratch_shapes=[
            pltpu.SMEM((own_len + ROWS,), jnp.int32),
            pltpu.VMEM((none + 8, wide), jnp.float32),
            pltpu.VMEM((ROWS // 8, 8, taps * wide), jnp.float32),
            pltpu.VMEM((ROWS // 8, 8, wide), jnp.float32),
            pltpu.VMEM((own_len, wide), jnp.float32),
            pltpu.VMEM((own_len, wide), jnp.float32),
        ],
        compiler_params=pltpu.CompilerParams(vmem_limit_bytes=48 * 1024 * 1024),
    )(flags, kernel_map.reshape(-1), interior_bricks, features, cotangent, left, right, stack)
    grad_weights = lax.psum(partial, "gx")
    return output, grad_features, grad_weights


def solution(mesh):
    placed = (
        P(None, ("groups", "gx")),
        P(None, ("groups", "gx")),
        P(),
        P(None, ("groups", "gx")),
        P(("groups", "gx")),
    )
    return jax.shard_map(
        per_device,
        mesh=mesh,
        in_specs=placed,
        out_specs=(P(None, ("groups", "gx")), P(None, ("groups", "gx")), P("groups", None, None)),
        check_vma=False,
    )
```

```python
import functools

import jax
import jax.numpy as jnp
from jax import lax
from jax.experimental import pallas as pl
from jax.experimental.pallas import tpu as pltpu
from jax.sharding import PartitionSpec as P

RB = 8
BRICK = 128
ROWS = 256


def gather_kernel(
    taps, channels, own_len, factor,
    flags, index, filled,
    feat, cot, left, right, stack,
    out_ref, gf_ref, gw_ref,
    picked, table, block, ups, compact, result, grads,
):
    rim_len = RB * BRICK
    wide = 2 * channels
    none = own_len + 2 * rim_len
    bricks = own_len // BRICK

    def fill_table(start, tile):
        table[pl.ds(start, BRICK), :] = tile.astype(jnp.float32).T

    for b in range(RB):
        cols = slice(b * BRICK, (b + 1) * BRICK)
        fill_table(b * BRICK, left[:, cols])
        fill_table(rim_len + own_len + b * BRICK, right[:, cols])
    table[pl.ds(none, 8), :] = jnp.zeros((8, wide), jnp.float32)
    result[...] = jnp.zeros_like(result)
    grads[...] = jnp.zeros_like(grads)

    def prepare(b, count):
        start = pl.multiple_of(b * BRICK, BRICK)
        cols = pl.ds(start, BRICK)
        live = (b < RB) | (b >= bricks - RB) | (b - RB < filled[0])
        up = jnp.where(live, cot[:, cols].astype(jnp.float32), 0.0)
        own = jnp.concatenate([feat[:, cols].astype(jnp.float32), up], axis=0)
        table[pl.ds(start + rim_len, BRICK), :] = own.T
        for j in range(BRICK):
            picked[count] = start + j
            count = count + flags[start + j]
        return count

    count = lax.fori_loop(0, bricks, prepare, 0)

    def pad(i, _):
        picked[count + i] = 0
        return _

    lax.fori_loop(0, ROWS, pad, 0)

    def visit(blk, _):
        base = blk * ROWS

        def fetch(step, _):
            for j in range(8):
                voxel = picked[base + step * 8 + j]
                ups[step, j : j + 1, :] = table[pl.ds(voxel + rim_len, 1), :]
                for k in range(taps):
                    source = index[k * own_len + voxel]
                    block[step, j : j + 1, k * wide : (k + 1) * wide] = table[pl.ds(source, 1), :]
            return _

        lax.fori_loop(0, ROWS // 8, fetch, 0)
        up = ups[...].reshape(ROWS, wide)
        row = lax.broadcasted_iota(jnp.int32, (ROWS, wide), 0)
        up = jnp.where(row + base < count, up, 0.0)
        up = up.T[channels:].astype(jnp.bfloat16)
        total = jnp.zeros((ROWS, wide), jnp.float32)
        for k in range(0, taps, 2):
            many = min(2, taps - k)
            cols = slice(k * wide, (k + many) * wide)
            part = block[:, :, cols].reshape(ROWS, many * wide).astype(jnp.bfloat16)
            total += jnp.dot(part, stack[cols, :], preferred_element_type=jnp.float32)
            grads[k // 2, :, : many * wide] += jnp.dot(
                up, part, preferred_element_type=jnp.float32
            )
        compact[pl.ds(pl.multiple_of(base, ROWS), ROWS), :] = total
        return _

    lax.fori_loop(0, (count + ROWS - 1) // ROWS, visit, 0)
    pairs = (taps + 1) // 2
    for p in range(pairs):
        both = grads[p] * factor
        gw_ref[p * channels : (p + 1) * channels, :] = jnp.concatenate(
            [both[:, :channels], both[:, wide : wide + channels]], axis=1
        )
    spare = gw_ref.shape[0] - pairs * channels
    if spare:
        gw_ref[pairs * channels :, :] = jnp.zeros((spare, wide), jnp.float32)

    def place(step, _):
        for j in range(8):
            at = step * 8 + j
            result[pl.ds(picked[at], 1), :] = compact[pl.ds(at, 1), :]
        return _

    lax.fori_loop(0, count // 8, place, 0)

    def place_one(at, _):
        result[pl.ds(picked[at], 1), :] = compact[pl.ds(at, 1), :]
        return _

    lax.fori_loop(count // 8 * 8, count, place_one, 0)

    for b in range(bricks):
        cols = slice(b * BRICK, (b + 1) * BRICK)
        both = result[cols, :].T
        if RB <= b < bricks - RB:
            both = jnp.where(b - RB < filled[0], both, 0.0)
        out_ref[:, cols] = both[:channels].astype(jnp.bfloat16)
        gf_ref[:, cols] = both[channels:].astype(jnp.bfloat16)


def sum_kernel(count, taps, channels, part, out, peer, mine, inbox, final, *sems):
    half = count // 2
    me = lax.axis_index("gx")
    chip, core = me // 2, me % 2
    twin = me + 1 - 2 * core
    near_send, near_recv, far_send, far_recv, all_send, all_recv, end_send, end_recv = sems

    def other(d):
        return ((chip + d) % half) * 2 + core

    def send(src, dst, send_sem, recv_sem, target):
        return pltpu.make_async_remote_copy(
            src_ref=src,
            dst_ref=dst,
            send_sem=send_sem,
            recv_sem=recv_sem,
            device_id={"gx": target},
            device_id_type=pl.DeviceIdType.MESH,
        )

    barrier = pltpu.get_barrier_semaphore()
    for target in [twin] + [other(d) for d in range(1, half)]:
        pl.semaphore_signal(
            barrier, inc=1, device_id={"gx": target}, device_id_type=pl.DeviceIdType.MESH
        )
    pl.semaphore_wait(barrier, half)

    order = list(range(1, half)) + [0]
    near = {}
    for d in order:
        t = (chip + d) % half
        near[d] = send(
            part.at[(1 - core) * half + t], peer.at[d], near_send.at[d], near_recv.at[d], twin
        )
        near[d].start()
    far = {}
    for d in order:
        t = (chip + d) % half
        near[d].wait_recv()
        mine[d] = part[core * half + t] + peer[d]
        if d:
            far[d] = send(mine.at[d], inbox.at[d], far_send.at[d], far_recv.at[d], other(d))
            far[d].start()
    total = mine[0]
    for d in range(1, half):
        far[d].wait_recv()
        total = total + inbox[d]
    slot = core * half + chip
    final[slot] = total
    ends = [send(final.at[slot], final.at[slot], end_send.at[0], end_recv.at[0], twin)]
    spread = {}
    for d in range(1, half):
        spread[d] = send(final.at[slot], final.at[slot], all_send.at[d], all_recv.at[d], other(d))
        spread[d].start()
    ends[0].start()
    for d in range(1, half):
        got = core * half + (chip + half - d) % half
        send(final.at[got], final.at[got], all_send.at[d], all_recv.at[d], twin).wait_recv()
        ends.append(send(final.at[got], final.at[got], end_send.at[d], end_recv.at[d], twin))
        ends[d].start()
    for d in range(half):
        ends[d].wait_recv()
    whole = final[...].reshape(-1, 2 * channels)
    for k in range(taps):
        tile = whole[k // 2 * channels : (k // 2 + 1) * channels]
        out[k] = tile[:, k % 2 * channels : (k % 2 + 1) * channels]
    for d in range(half):
        near[d].wait_send()
        ends[d].wait_send()
        if d:
            far[d].wait_send()
            spread[d].wait_send()


def sum_over_gx(part, taps, channels):
    count, share, wide = part.shape
    half = count // 2
    vmem = pl.BlockSpec(memory_space=pltpu.VMEM)
    return pl.pallas_call(
        functools.partial(sum_kernel, count, taps, channels),
        out_shape=jax.ShapeDtypeStruct((taps, channels, channels), jnp.float32),
        in_specs=[vmem],
        out_specs=vmem,
        scratch_shapes=[pltpu.VMEM((half, share, wide), jnp.float32)] * 3
        + [pltpu.VMEM((count, share, wide), jnp.float32)]
        + [pltpu.SemaphoreType.DMA((half,))] * 8,
        compiler_params=pltpu.CompilerParams(
            collective_id=0, has_side_effects=True, vmem_limit_bytes=16 * 1024 * 1024
        ),
    )(part)


def per_device(features, cotangent, weights, kernel_map, interior_bricks):
    channels, own_len = features.shape
    taps = weights.shape[0]
    rim_len = RB * BRICK
    wide = 2 * channels
    count = lax.axis_size("gx")
    none = own_len + 2 * rim_len
    factor = float(count * own_len) ** (-0.5)

    tail = jnp.concatenate([features[:, own_len - rim_len :], cotangent[:, own_len - rim_len :]], 0)
    head = jnp.concatenate([features[:, :rim_len], cotangent[:, :rim_len]], 0)
    left = lax.ppermute(tail, "gx", [(i, i + 1) for i in range(count - 1)])
    right = lax.ppermute(head, "gx", [(i + 1, i) for i in range(count - 1)])
    flags = jnp.any(kernel_map != none, axis=0).astype(jnp.int32)
    share = -(-((taps + 1) // 2 * channels) // (8 * count)) * 8
    rows = count * share
    zero = jnp.zeros_like(weights)
    stack = jnp.concatenate(
        [
            jnp.concatenate([jnp.transpose(weights, (0, 2, 1)), zero], 2),
            jnp.concatenate([zero, weights[::-1]], 2),
        ],
        1,
    ).reshape(taps * wide, wide)
    smem = pl.BlockSpec(memory_space=pltpu.SMEM)
    vmem = pl.BlockSpec(memory_space=pltpu.VMEM)
    output, grad_features, partial = pl.pallas_call(
        functools.partial(gather_kernel, taps, channels, own_len, factor),
        out_shape=(
            jax.ShapeDtypeStruct((channels, own_len), jnp.bfloat16),
            jax.ShapeDtypeStruct((channels, own_len), jnp.bfloat16),
            jax.ShapeDtypeStruct((rows, wide), jnp.float32),
        ),
        in_specs=[smem] * 3 + [vmem] * 5,
        out_specs=(vmem,) * 3,
        scratch_shapes=[
            pltpu.SMEM((own_len + ROWS,), jnp.int32),
            pltpu.VMEM((none + 8, wide), jnp.float32),
            pltpu.VMEM((ROWS // 8, 8, taps * wide), jnp.float32),
            pltpu.VMEM((ROWS // 8, 8, wide), jnp.float32),
            pltpu.VMEM((own_len, wide), jnp.float32),
            pltpu.VMEM((own_len, wide), jnp.float32),
            pltpu.VMEM(((taps + 1) // 2, channels, 2 * wide), jnp.float32),
        ],
        compiler_params=pltpu.CompilerParams(vmem_limit_bytes=48 * 1024 * 1024),
    )(flags, kernel_map.reshape(-1), interior_bricks, features, cotangent, left, right, stack)
    grad_weights = sum_over_gx(partial.reshape(count, rows // count, wide), taps, channels)
    return output, grad_features, grad_weights


def solution(mesh):
    placed = (
        P(None, ("groups", "gx")),
        P(None, ("groups", "gx")),
        P(),
        P(None, ("groups", "gx")),
        P(("groups", "gx")),
    )
    return jax.shard_map(
        per_device,
        mesh=mesh,
        in_specs=placed,
        out_specs=(P(None, ("groups", "gx")), P(None, ("groups", "gx")), P("groups", None, None)),
        check_vma=False,
    )
```

```python
import functools

import jax
import jax.numpy as jnp
from jax import lax
from jax.experimental import pallas as pl
from jax.experimental.pallas import tpu as pltpu
from jax.sharding import PartitionSpec as P

RB = 8
BRICK = 128
ROWS = 256


def list_kernel(own_len, flags, picked, many):
    def note(step, count):
        start = step * BRICK
        for j in range(BRICK):
            picked[count] = start + j
            count = count + flags[start + j]
        return count

    count = lax.fori_loop(0, own_len // BRICK, note, 0)

    def pad(step, _):
        for j in range(32):
            picked[count + step * 32 + j] = 0
        return _

    lax.fori_loop(0, ROWS // 32, pad, 0)
    many[0] = count


def gather_kernel(
    taps, channels, own_len, factor,
    picked, many, index, filled,
    feat, cot, left, right, stack,
    out_ref, gf_ref, gw_ref,
    table, block, ups, compact, result, grads,
):
    rim_len = RB * BRICK
    wide = 2 * channels
    none = own_len + 2 * rim_len
    bricks = own_len // BRICK

    def fill_table(start, tile):
        table[pl.ds(start, BRICK), :] = tile.astype(jnp.float32).T

    for b in range(RB):
        cols = slice(b * BRICK, (b + 1) * BRICK)
        fill_table(b * BRICK, left[:, cols])
        fill_table(rim_len + own_len + b * BRICK, right[:, cols])
    table[pl.ds(none, 8), :] = jnp.zeros((8, wide), jnp.float32)
    result[...] = jnp.zeros_like(result)
    grads[...] = jnp.zeros_like(grads)

    def prepare(b, _):
        start = pl.multiple_of(b * BRICK, BRICK)
        cols = pl.ds(start, BRICK)
        live = (b < RB) | (b >= bricks - RB) | (b - RB < filled[0])
        up = jnp.where(live, cot[:, cols].astype(jnp.float32), 0.0)
        own = jnp.concatenate([feat[:, cols].astype(jnp.float32), up], axis=0)
        table[pl.ds(start + rim_len, BRICK), :] = own.T
        return _

    lax.fori_loop(0, bricks, prepare, 0)
    count = many[0]

    def visit(blk, _):
        base = blk * ROWS

        def fetch(step, _):
            sources = []
            for j in range(8):
                voxel = picked[base + step * 8 + j]
                ups[step, j : j + 1, :] = table[pl.ds(voxel + rim_len, 1), :]
                sources.append(index.at[pl.ds(voxel, (taps - 1) * own_len + 1)])
            for k in range(taps):
                for j in range(8):
                    source = sources[j][k * own_len]
                    block[step, j : j + 1, k * wide : (k + 1) * wide] = table[pl.ds(source, 1), :]
            return _

        lax.fori_loop(0, ROWS // 8, fetch, 0)
        up = ups[...].reshape(ROWS, wide)
        row = lax.broadcasted_iota(jnp.int32, (ROWS, wide), 0)
        up = jnp.where(row + base < count, up, 0.0)
        up = up.T[channels:].astype(jnp.bfloat16)
        total = jnp.zeros((ROWS, wide), jnp.float32)
        for k in range(0, taps, 2):
            both = min(2, taps - k)
            cols = slice(k * wide, (k + both) * wide)
            part = block[:, :, cols].reshape(ROWS, both * wide).astype(jnp.bfloat16)
            total += jnp.dot(part, stack[cols, :], preferred_element_type=jnp.float32)
            grads[k // 2, :, : both * wide] += jnp.dot(
                up, part, preferred_element_type=jnp.float32
            )
        compact[pl.ds(pl.multiple_of(base, ROWS), ROWS), :] = total
        return _

    lax.fori_loop(0, (count + ROWS - 1) // ROWS, visit, 0)
    pairs = (taps + 1) // 2
    for p in range(pairs):
        both = grads[p] * factor
        gw_ref[p * channels : (p + 1) * channels, :] = jnp.concatenate(
            [both[:, :channels], both[:, wide : wide + channels]], axis=1
        )
    spare = gw_ref.shape[0] - pairs * channels
    if spare:
        gw_ref[pairs * channels :, :] = jnp.zeros((spare, wide), jnp.float32)

    def place(step, _):
        for j in range(8):
            at = step * 8 + j
            result[pl.ds(picked[at], 1), :] = compact[pl.ds(at, 1), :]
        return _

    lax.fori_loop(0, count // 8, place, 0)

    def place_one(at, _):
        result[pl.ds(picked[at], 1), :] = compact[pl.ds(at, 1), :]
        return _

    lax.fori_loop(count // 8 * 8, count, place_one, 0)

    for b in range(bricks):
        cols = slice(b * BRICK, (b + 1) * BRICK)
        both = result[cols, :].T
        if RB <= b < bricks - RB:
            both = jnp.where(b - RB < filled[0], both, 0.0)
        out_ref[:, cols] = both[:channels].astype(jnp.bfloat16)
        gf_ref[:, cols] = both[channels:].astype(jnp.bfloat16)


def sum_kernel(count, taps, channels, part, out, peer, mine, inbox, final, *sems):
    half = count // 2
    me = lax.axis_index("gx")
    chip, core = me // 2, me % 2
    twin = me + 1 - 2 * core
    near_send, near_recv, far_send, far_recv, all_send, all_recv, end_send, end_recv = sems

    def other(d):
        return ((chip + d) % half) * 2 + core

    def send(src, dst, send_sem, recv_sem, target):
        return pltpu.make_async_remote_copy(
            src_ref=src,
            dst_ref=dst,
            send_sem=send_sem,
            recv_sem=recv_sem,
            device_id={"gx": target},
            device_id_type=pl.DeviceIdType.MESH,
        )

    barrier = pltpu.get_barrier_semaphore()
    for target in [twin] + [other(d) for d in range(1, half)]:
        pl.semaphore_signal(
            barrier, inc=1, device_id={"gx": target}, device_id_type=pl.DeviceIdType.MESH
        )
    pl.semaphore_wait(barrier, half)

    order = list(range(1, half)) + [0]
    near = {}
    for d in order:
        t = (chip + d) % half
        near[d] = send(
            part.at[(1 - core) * half + t], peer.at[d], near_send.at[d], near_recv.at[d], twin
        )
        near[d].start()
    far = {}
    for d in order:
        t = (chip + d) % half
        near[d].wait_recv()
        mine[d] = part[core * half + t] + peer[d]
        if d:
            far[d] = send(mine.at[d], inbox.at[d], far_send.at[d], far_recv.at[d], other(d))
            far[d].start()
    total = mine[0]
    for d in range(1, half):
        far[d].wait_recv()
        total = total + inbox[d]
    slot = core * half + chip
    final[slot] = total
    ends = [send(final.at[slot], final.at[slot], end_send.at[0], end_recv.at[0], twin)]
    spread = {}
    for d in range(1, half):
        spread[d] = send(final.at[slot], final.at[slot], all_send.at[d], all_recv.at[d], other(d))
        spread[d].start()
    ends[0].start()
    for d in range(1, half):
        got = core * half + (chip + half - d) % half
        send(final.at[got], final.at[got], all_send.at[d], all_recv.at[d], twin).wait_recv()
        ends.append(send(final.at[got], final.at[got], end_send.at[d], end_recv.at[d], twin))
        ends[d].start()
    for d in range(half):
        ends[d].wait_recv()
    whole = final[...].reshape(-1, 2 * channels)
    for k in range(taps):
        tile = whole[k // 2 * channels : (k // 2 + 1) * channels]
        out[k] = tile[:, k % 2 * channels : (k % 2 + 1) * channels]
    for d in range(half):
        near[d].wait_send()
        ends[d].wait_send()
        if d:
            far[d].wait_send()
            spread[d].wait_send()


def sum_over_gx(part, taps, channels):
    count, share, wide = part.shape
    half = count // 2
    vmem = pl.BlockSpec(memory_space=pltpu.VMEM)
    return pl.pallas_call(
        functools.partial(sum_kernel, count, taps, channels),
        out_shape=jax.ShapeDtypeStruct((taps, channels, channels), jnp.float32),
        in_specs=[vmem],
        out_specs=vmem,
        scratch_shapes=[pltpu.VMEM((half, share, wide), jnp.float32)] * 3
        + [pltpu.VMEM((count, share, wide), jnp.float32)]
        + [pltpu.SemaphoreType.DMA((half,))] * 8,
        compiler_params=pltpu.CompilerParams(
            collective_id=0, has_side_effects=True, vmem_limit_bytes=16 * 1024 * 1024
        ),
    )(part)


def per_device(features, cotangent, weights, kernel_map, interior_bricks):
    channels, own_len = features.shape
    taps = weights.shape[0]
    rim_len = RB * BRICK
    wide = 2 * channels
    count = lax.axis_size("gx")
    none = own_len + 2 * rim_len
    factor = float(count * own_len) ** (-0.5)

    tail = jnp.concatenate([features[:, own_len - rim_len :], cotangent[:, own_len - rim_len :]], 0)
    head = jnp.concatenate([features[:, :rim_len], cotangent[:, :rim_len]], 0)
    left = lax.ppermute(tail, "gx", [(i, i + 1) for i in range(count - 1)])
    right = lax.ppermute(head, "gx", [(i + 1, i) for i in range(count - 1)])
    flags = jnp.any(kernel_map != none, axis=0).astype(jnp.int32)
    share = -(-((taps + 1) // 2 * channels) // (8 * count)) * 8
    rows = count * share
    zero = jnp.zeros_like(weights)
    stack = jnp.concatenate(
        [
            jnp.concatenate([jnp.transpose(weights, (0, 2, 1)), zero], 2),
            jnp.concatenate([zero, weights[::-1]], 2),
        ],
        1,
    ).reshape(taps * wide, wide)
    smem = pl.BlockSpec(memory_space=pltpu.SMEM)
    vmem = pl.BlockSpec(memory_space=pltpu.VMEM)
    picked, many = pl.pallas_call(
        functools.partial(list_kernel, own_len),
        out_shape=(
            jax.ShapeDtypeStruct((own_len + ROWS,), jnp.int32),
            jax.ShapeDtypeStruct((1,), jnp.int32),
        ),
        in_specs=[smem],
        out_specs=(smem, smem),
        cost_estimate=pl.CostEstimate(
            flops=own_len * 2048, bytes_accessed=own_len * 2048, transcendentals=0
        ),
    )(flags)
    output, grad_features, partial = pl.pallas_call(
        functools.partial(gather_kernel, taps, channels, own_len, factor),
        out_shape=(
            jax.ShapeDtypeStruct((channels, own_len), jnp.bfloat16),
            jax.ShapeDtypeStruct((channels, own_len), jnp.bfloat16),
            jax.ShapeDtypeStruct((rows, wide), jnp.float32),
        ),
        in_specs=[smem] * 4 + [vmem] * 5,
        out_specs=(vmem,) * 3,
        scratch_shapes=[
            pltpu.VMEM((none + 8, wide), jnp.float32),
            pltpu.VMEM((ROWS // 8, 8, taps * wide), jnp.float32),
            pltpu.VMEM((ROWS // 8, 8, wide), jnp.float32),
            pltpu.VMEM((own_len, wide), jnp.float32),
            pltpu.VMEM((own_len, wide), jnp.float32),
            pltpu.VMEM(((taps + 1) // 2, channels, 2 * wide), jnp.float32),
        ],
        compiler_params=pltpu.CompilerParams(vmem_limit_bytes=48 * 1024 * 1024),
    )(picked, many, kernel_map.reshape(-1), interior_bricks, features, cotangent, left, right, stack)
    grad_weights = sum_over_gx(partial.reshape(count, rows // count, wide), taps, channels)
    return output, grad_features, grad_weights


def solution(mesh):
    placed = (
        P(None, ("groups", "gx")),
        P(None, ("groups", "gx")),
        P(),
        P(None, ("groups", "gx")),
        P(("groups", "gx")),
    )
    return jax.shard_map(
        per_device,
        mesh=mesh,
        in_specs=placed,
        out_specs=(P(None, ("groups", "gx")), P(None, ("groups", "gx")), P("groups", None, None)),
        check_vma=False,
    )
```
